128 devices in a mesh: dp: 8 (over x, core), mp: 16 (over z, y).
Axes of the slice: x: 4, y: 4, z: 4, core: 2. Of those that a mesh axis runs over, the one named last changes fastest.
Arguments:
- q_new: bfloat16 [1024, 8192], P(('dp', 'mp')), may hold values from -9 to 9
- k_new: bfloat16 [1024, 1024], P(('dp', 'mp')), may hold values from -9 to 9
- v_new: bfloat16 [1024, 1024], P(('dp', 'mp')), may hold values from -6 to 6
- suffix_keys: bfloat16 [1024, 128, 1024], P(('dp', 'mp')), may hold values from -12 to 12
- suffix_values: bfloat16 [1024, 128, 1024], P(('dp', 'mp')), may hold values from -6 to 6
- suffix_len: int32 [1024], P(('dp', 'mp')), may hold values from 1 to 128, 81920 in all
- prefix_keys: bfloat16 [8, 8192, 1024], P('dp', 'mp'), may hold values from -12 to 12
- prefix_values: bfloat16 [8, 8192, 1024], P('dp', 'mp'), may hold values from -6 to 6
- prefix_len: int32 [8], replicated, may hold values from 1 to 8192, 36864 in all
- sample_prompt: int32 [1024], P(('dp', 'mp')), may hold values from 0 to 7, as said below
- out_weight: bfloat16 [8192, 5120], P('mp'), may hold values from -0.0625 to 0.0625
Outputs:
- attn_out: bfloat16 [1024, 5120], P(('dp', 'mp'))
The draws below stay inside these ranges and needn't reach their ends.
Inputs may be any that keep to these rules, and one draw needn't show every extreme that they name: `sample_prompt`: in each aligned block of 8 rows (the samples of one device) at most 2 samples belong to one prompt, and one prompt, the same in every block, has exactly 2 there. `prefix_len`: the longest prefix is exactly 8192. `suffix_len`: the longest suffix is exactly 128.
All inputs are finite; a program needn't handle non-finite values. No bound on the sum of `suffix_len` on one device may be relied on, other than what follows from the above.
Results may differ from the reference program's by a relative error of at most 0.005.
Values may be sent and summed in bfloat16 or wider, within the bound.
A program may use at most 320 MiB of HBM per device.

```python
import math
import jax
import jax.numpy as jnp
import numpy as np
from jax import lax

H = 64
KVH = 8
HD = 128
D = 5120
S_LOC = 8
SUF = 128
KB = 256
CAP = 2
PROMPTS = 8
SAMPLES = 1024
PREFIX = 8192


def base_queries(key):
    normals = jax.random.normal(jax.random.fold_in(key, 800), (SAMPLES, H * HD), jnp.float32)
    return jnp.clip(1.5 * normals, -9.0, 9.0)


def draw_q_new(key, part):
    queries = base_queries(key)
    return queries.astype(jnp.bfloat16)


def draw_k_new(key, part):
    queries = base_queries(key)
    key = jax.random.fold_in(key, 41)
    grouped = queries.reshape(SAMPLES, KVH, H // KVH, HD).mean(axis=2)
    noise = jax.random.normal(key, (SAMPLES, KVH, HD), jnp.float32)
    return jnp.clip(4.0 * grouped + noise, -9.0, 9.0).reshape(SAMPLES, KVH * HD).astype(jnp.bfloat16)


def draw_prefix_keys(key, part):
    key = jax.random.fold_in(key, 21)
    entries = 2.0 * jax.random.normal(key, (PROMPTS, PREFIX, KVH * HD), jnp.float32)
    return jnp.clip(entries, -12.0, 12.0).astype(jnp.bfloat16)


def draw_sample_prompt(key, part):
    key = jax.random.fold_in(key, 5)
    block_total = SAMPLES // S_LOC
    crowded = jax.random.randint(jax.random.fold_in(key, 1), (), 0, PROMPTS).astype(jnp.int32)
    others = ((crowded + 1 + jnp.arange(PROMPTS - 1)) % PROMPTS).astype(jnp.int32)
    spares = jnp.repeat(others, CAP)
    block_keys = jax.random.split(jax.random.fold_in(key, 2), block_total)

    def one_block(block_key):
        pick_key, order_key = jax.random.split(block_key)
        picked = jax.random.permutation(pick_key, spares)[:S_LOC - CAP]
        block_rows = jnp.concatenate([jnp.full((CAP,), crowded, jnp.int32), picked.astype(jnp.int32)])
        return jax.random.permutation(order_key, block_rows)
    return jax.vmap(one_block)(block_keys).reshape(SAMPLES).astype(jnp.int32)


def shard_levels(key, extent, shards, low, largest):
    def one(axis_at, parts):
        steps = jax.random.uniform(jax.random.fold_in(jax.random.fold_in(key, 6), axis_at), (parts,), jnp.float32, low / len(shards), largest / len(shards))
        return jnp.repeat(jnp.exp(steps), extent[axis_at] // parts).reshape((-1,) + (1,) * (len(extent) - axis_at - 1))

    factor_of = one(*shards[0])
    for cut in shards[1:]:
        factor_of = factor_of * one(*cut)
    return factor_of


def profile(number_of, total, limit, lean):
    weights = [(1 << 20) // math.isqrt(rank ** lean) + 1 for rank in range(2, number_of + 1)]
    rest, holding = total - limit - (number_of - 1), [1] * (number_of - 1)
    while rest > 0:
        candidates = [i for i in range(number_of - 1) if holding[i] < limit]
        whole, budget = sum([weights[i] for i in candidates]), rest
        for i in candidates:
            extra = min(limit - holding[i], max(1, budget * weights[i] // whole), rest)
            holding[i] = holding[i] + extra
            rest = rest - extra
    return np.array([limit] + holding)


def uneven(key, number_of, total, bound, slope):
    if number_of == 2:
        one = jax.random.randint(key, (), max(1, total - bound), min(bound, total - 1) + 1)
        return jnp.stack([one, total - one])
    sizes = jnp.asarray(profile(number_of, total, bound, slope), jnp.int32)
    twos = (number_of - 1) // 2
    donor, taker = sizes[1:1 + 2 * twos:2], sizes[2:2 + 2 * twos:2]
    margin = jnp.minimum(donor - 1, bound - taker)
    moved = jax.random.randint(jax.random.fold_in(key, 1), (twos,), 0, 1 << 20) % (margin + 1)
    sizes = sizes.at[1:1 + 2 * twos:2].set(donor - moved).at[2:2 + 2 * twos:2].set(taker + moved)
    return sizes[jax.random.permutation(jax.random.fold_in(key, 2), number_of)]


def scatter_about(key, shape, scale, most, shards=(), held_as=jnp.bfloat16):
    result = scale * jax.random.normal(key, shape, jnp.float32)
    if shards:
        result = result * shard_levels(key, shape, shards, -0.22, 0.18)
    return jnp.clip(result, -most, most).astype(held_as)


def setup_inputs(seed: int = 0) -> dict:
    keys = jax.random.split(jax.random.key(seed), 12)
    q_new = draw_q_new(jax.random.fold_in(keys[11], 71), 0)
    k_new = draw_k_new(jax.random.fold_in(keys[11], 71), 0)
    v_new = scatter_about(keys[2], (SAMPLES, KVH * HD), 1.0, 6.0, ((0, 128),))
    suffix_keys = scatter_about(keys[3], (SAMPLES, SUF, KVH * HD), 2.0, 12.0, ((0, 128),))
    suffix_values = scatter_about(keys[4], (SAMPLES, SUF, KVH * HD), 1.0, 6.0, ((0, 128),))
    suffix_len = uneven(keys[5], SAMPLES, SAMPLES * SUF * 5 // 8, SUF, 1).astype(jnp.int32)
    prefix_keys = draw_prefix_keys(jax.random.fold_in(keys[11], 71), 0)
    prefix_values = scatter_about(keys[7], (PROMPTS, PREFIX, KVH * HD), 1.0, 6.0, ((0, 8), (1, 16)))
    prefix_len = uneven(keys[8], PROMPTS, PREFIX * (PROMPTS + 1) // 2, PREFIX, 1).astype(jnp.int32)
    sample_prompt = draw_sample_prompt(jax.random.fold_in(keys[11], 71), 0)
    out_weight = scatter_about(keys[10], (H * HD, D), (H * HD) ** -0.5, 0.0625, ((0, 16),))
    return {"q_new": q_new, "k_new": k_new, "v_new": v_new, "suffix_keys": suffix_keys, "suffix_values": suffix_values, "suffix_len": suffix_len, "prefix_keys": prefix_keys, "prefix_values": prefix_values, "prefix_len": prefix_len, "sample_prompt": sample_prompt, "out_weight": out_weight}


NEG_FILL = -1e30


def reference(q_new, k_new, v_new, suffix_keys, suffix_values, suffix_len, prefix_keys, prefix_values, prefix_len, sample_prompt, out_weight):
    per_group = H // KVH
    score_scale = HD ** -0.5
    block_count = PREFIX // KB
    owner_rows = sample_prompt.astype(jnp.int32)
    lengths = prefix_len[sample_prompt].astype(jnp.int32)

    def one_sample(inputs):
        query_row, own_key, own_value, cache_keys, cache_values, suffix_count, owner_row, prefix_count = inputs
        query32 = query_row.astype(jnp.float32).reshape(KVH, per_group, HD)
        key_rows = lax.dynamic_index_in_dim(prefix_keys, owner_row, 0, keepdims=False).astype(jnp.float32).reshape(PREFIX, KVH, HD)
        value_rows = lax.dynamic_index_in_dim(prefix_values, owner_row, 0, keepdims=False).astype(jnp.float32).reshape(block_count, KB, KVH, HD)
        scores = jnp.einsum("kgd,jkd->kgj", query32, key_rows, precision=lax.Precision.HIGHEST) * score_scale
        scores = scores.reshape(KVH, per_group, block_count, KB)
        is_valid = (jnp.arange(PREFIX) < prefix_count).reshape(block_count, KB)
        masked = jnp.where(is_valid, scores, NEG_FILL)
        block_max = masked.max(axis=-1)
        weights = jnp.where(is_valid, jnp.exp(masked - block_max[..., None]), 0.0)
        block_total = weights.sum(axis=-1)
        rounded = lax.optimization_barrier(weights.astype(jnp.bfloat16)).astype(jnp.float32)
        block_acc = jnp.einsum("kgbj,bjkd->kgbd", rounded, value_rows, precision=lax.Precision.HIGHEST)

        cache_k32 = cache_keys.astype(jnp.float32).reshape(SUF, KVH, HD)
        cache_v32 = cache_values.astype(jnp.float32).reshape(SUF, KVH, HD)
        suffix_scores = jnp.einsum("kgd,jkd->kgj", query32, cache_k32, precision=lax.Precision.HIGHEST) * score_scale
        self_score = jnp.einsum("kgd,kd->kg", query32, own_key.astype(jnp.float32).reshape(KVH, HD), precision=lax.Precision.HIGHEST) * score_scale
        suffix_valid = jnp.arange(SUF) < suffix_count
        suffix_masked = jnp.where(suffix_valid, suffix_scores, NEG_FILL)
        suffix_max = jnp.maximum(suffix_masked.max(axis=-1), self_score)
        suffix_weights = jnp.where(suffix_valid, jnp.exp(suffix_masked - suffix_max[..., None]), 0.0)
        self_weight = jnp.exp(self_score - suffix_max)
        suffix_total = suffix_weights.sum(axis=-1) + self_weight
        suffix_rounded = lax.optimization_barrier(suffix_weights.astype(jnp.bfloat16)).astype(jnp.float32)
        self_rounded = lax.optimization_barrier(self_weight.astype(jnp.bfloat16)).astype(jnp.float32)
        suffix_acc = jnp.einsum("kgj,jkd->kgd", suffix_rounded, cache_v32, precision=lax.Precision.HIGHEST)
        suffix_acc = suffix_acc + self_rounded[..., None] * own_value.astype(jnp.float32).reshape(KVH, 1, HD)

        overall_max = jnp.maximum(block_max.max(axis=-1), suffix_max)
        block_factor = jnp.exp(block_max - overall_max[..., None])
        suffix_factor = jnp.exp(suffix_max - overall_max)
        denominator = (block_total * block_factor).sum(axis=-1) + suffix_total * suffix_factor
        numerator = (block_acc * block_factor[..., None]).sum(axis=2) + suffix_acc * suffix_factor[..., None]
        return (numerator / denominator[..., None]).reshape(H * HD).astype(jnp.bfloat16)

    attention = lax.map(one_sample, (q_new, k_new, v_new, suffix_keys, suffix_values, suffix_len, owner_rows, lengths))
    return jnp.dot(attention, out_weight, preferred_element_type=jnp.float32).astype(jnp.bfloat16)
```

```python
import functools
import math

import jax
import jax.numpy as jnp
from jax import lax
from jax.experimental import pallas as pl
from jax.experimental.pallas import tpu as pltpu
from jax.sharding import PartitionSpec as P

H = 64
KVH = 8
G = H // KVH
HD = 128
CAP = 2
S_LOC = 8
NM = 16
KW = G * HD
NEG = -1e30
FLOOR = -1e28
SCALE2 = HD ** (-0.5) * math.log2(math.e)
SLOT_ORDER = (0, 1, 2, 3, 6, 7, 4, 5)
F32 = jnp.float32
BF16 = jnp.bfloat16
MESH = pl.DeviceIdType.MESH

NT = (((1,), (1,)), ((), ()))
TN = (((0,), (0,)), ((), ()))


def dot(a, b, dims=(((1,), (0,)), ((), ()))):
    return lax.dot_general(a, b, dims, preferred_element_type=F32)


def iota(shape, dim):
    return lax.broadcasted_iota(jnp.int32, shape, dim)


def pieces(value):
    high = value.astype(BF16).astype(F32)
    rest = value - high
    mid = rest.astype(BF16).astype(F32)
    low = (rest - mid).astype(BF16).astype(F32)
    return high, mid, low


def kernel(
    nd, slen_ref, plen_ref, sp_ref, q_ref, kn_ref, vn_ref, sk_ref, sv_ref, pk_ref, pv_ref, w_ref,
    out_ref,
    kx, vx, w, kr, vr, vt, q1s, q1, qk, q2s, q2, sel, acc, stat_m, stat_l, lse, resm, rres,
    sfxs, sfx, att, part, rsb, bias,
    local_sem, kv_send, kv_recv, q1_send, q1_recv, q2_send, q2_recv, sf_send, sf_recv,
    re_send, re_recv, rs_send, rs_recv,
):
    d = lax.axis_index("dp")
    m = lax.axis_index("mp")
    z, y = m // 4, m % 4
    k, h = m // 2, m % 2
    partner = m + 1 - 2 * h
    suf = sk_ref.shape[0] // S_LOC
    rows_own = S_LOC * suf
    rows_x = kx.shape[0]
    chunk = pk_ref.shape[0]
    nslot = nd * NM * CAP

    barrier = pltpu.get_barrier_semaphore()

    def greet(dd, mm):
        pl.semaphore_signal(barrier, inc=1, device_id=(dd, mm), device_id_type=MESH)

    def greet_mp(j, c):
        greet(d, (m + j) % NM)
        return c

    def greet_dp(j, c):
        greet((d + j) % nd, m)
        greet((d + j) % nd, partner)
        return c

    lax.fori_loop(1, NM, greet_mp, 0)
    lax.fori_loop(1, nd, greet_dp, 0)

    cols = pl.ds(pl.multiple_of(k * HD, HD), HD)
    own_k = pltpu.make_async_copy(pk_ref.at[:, cols], kr.at[0], local_sem.at[0])
    own_v = pltpu.make_async_copy(pv_ref.at[:, cols], vr.at[0], local_sem.at[1])
    copy_sk = pltpu.make_async_copy(sk_ref, kx.at[pl.ds(0, rows_own)], local_sem.at[2])
    copy_sv = pltpu.make_async_copy(sv_ref, vx.at[pl.ds(0, rows_own)], local_sem.at[3])
    copy_w = pltpu.make_async_copy(w_ref, w, local_sem.at[4])
    for c in (own_k, own_v, copy_sk, copy_sv, copy_w):
        c.start()

    prompts = [sp_ref[i] for i in range(S_LOC)]
    targets = []
    for i in range(S_LOC):
        rank = jnp.int32(0)
        for j in range(i):
            rank = rank + jnp.where(prompts[j] == prompts[i], 1, 0)
        targets.append(prompts[i] * (NM * CAP) + m * CAP + rank)
    row16 = iota((16, 128), 0) % S_LOC
    target16 = jnp.zeros((16, 128), jnp.int32)
    for i in range(S_LOC):
        target16 = jnp.where(row16 == i, targets[i], target16)
    target16 = target16.astype(F32)

    for kk in range(KVH):
        block = q_ref[:, kk * KW:(kk + 1) * KW].astype(F32)
        both = jnp.concatenate([block[:, : KW // 2], block[:, KW // 2:]], axis=0)
        q1s[kk, :, 0: KW // 2] = both.astype(BF16)
        q1s[kk, :, KW // 2:] = target16.astype(BF16)
        heads = jnp.concatenate([block[:, g * HD:(g + 1) * HD] for g in range(G)], axis=0)
        qk[kk] = heads.astype(BF16)
    q1[m] = q1s[k]

    pl.semaphore_wait(barrier, NM - 1 + 2 * (nd - 1))

    def q1_copy(j):
        mm = (m + j) % NM
        return pltpu.make_async_remote_copy(
            q1s.at[mm // 2], q1.at[m], q1_send.at[j], q1_recv.at[m],
            device_id=(d, mm), device_id_type=MESH)

    def q1_arrival(j):
        mm = (m + j) % NM
        return pltpu.make_async_remote_copy(
            q1s.at[0], q1.at[mm], q1_send.at[j], q1_recv.at[mm],
            device_id=(d, mm), device_id_type=MESH)

    def run(lo, hi, body):
        def step(j, c):
            body(j)
            return c
        lax.fori_loop(lo, hi, step, 0)

    run(1, NM, lambda j: q1_copy(j).start())

    kv_copies = []
    for n, (tz, t) in enumerate([(0, 1), (1, 0), (1, 1), (3, 0), (3, 1), (2, 0), (2, 1)]):
        zz = (z + tz) % 4
        pair = (y // 2 + t) % 2
        kk = 2 * zz + pair
        rel = (y + 4 - 2 * pair) % 4
        yy = 2 * pair + ((rel + 1) // 2) % 2
        flag = (yy + 4 - y) % 2
        slot = 2 * ((4 - tz) % 4) + flag
        src_cols = pl.ds(pl.multiple_of(kk * HD, HD), HD)
        for a, (src, dst) in enumerate(((pk_ref, kr), (pv_ref, vr))):
            kv_copies.append(pltpu.make_async_remote_copy(
                src.at[:, src_cols], dst.at[slot], kv_send.at[n, a], kv_recv.at[slot, a],
                device_id=(d, 4 * zz + yy), device_id_type=MESH))
    for c in kv_copies:
        c.start()

    pad = jnp.zeros((rows_x - rows_own - S_LOC, KW), F32)
    copy_sk.wait()
    copy_sv.wait()
    kx[rows_own:, :] = jnp.concatenate([kn_ref[...].astype(F32), pad], axis=0).astype(BF16)
    vx[rows_own:, :] = jnp.concatenate([vn_ref[...].astype(F32), pad], axis=0).astype(BF16)
    lane_sample = iota((suf, 64), 1) % S_LOC
    position = iota((suf, 64), 0)
    for i in range(S_LOC):
        good = jnp.logical_and(lane_sample == i, position < slen_ref[i])
        bias[i * suf:(i + 1) * suf, :] = jnp.where(good, 0.0, NEG)
    tail = (rows_x - rows_own, 64)
    bias[rows_own:, :] = jnp.where(iota(tail, 0) == iota(tail, 1) % S_LOC, 0.0, NEG)
    eye64 = (iota((64, 64), 0) == iota((64, 64), 1)).astype(BF16)

    def suffix_head(kk):
        at = pl.ds(pl.multiple_of(kk * HD, HD), HD)
        scores = dot(kx[:, at], qk[kk], NT) * SCALE2 + bias[...]
        top = jnp.max(scores, axis=0, keepdims=True)
        weights = jnp.exp2(scores - top)
        total = jnp.sum(weights, axis=0, keepdims=True)
        mean = dot(vx[:, at], weights.astype(BF16), TN) / total
        high, mid, low = pieces(top + jnp.log2(total))
        row = iota((HD, 64), 0)
        extra = jnp.where(row == 0, high, jnp.where(row == 1, mid, jnp.where(row == 2, low, 0.0)))
        both = jnp.concatenate([mean, extra], axis=0).astype(BF16)
        turned = dot(eye64, both, NT).astype(BF16)
        sfxs[2 * kk] = turned[:32]
        sfxs[2 * kk + 1] = turned[32:]

    run(0, KVH // 2, suffix_head)

    run(1, NM, lambda j: q1_arrival(j).wait_recv())
    arrived = q1[...].astype(F32).reshape(NM, 2, S_LOC, KW // 2 + 128)
    at_slot = arrived[:, 0, :, KW // 2:].reshape(NM * S_LOC, 128)
    lane = iota((NM * S_LOC, 128), 1)
    for part_at in range(nslot // 128):
        sel[:, part_at * 128:(part_at + 1) * 128] = (
            at_slot == (lane + part_at * 128).astype(F32)).astype(F32).astype(BF16)
    for half in range(2):
        mine = arrived[:, half, :, : KW // 2].reshape(NM * S_LOC, KW // 2).astype(BF16)
        placed = dot(sel[...], mine, TN).astype(BF16)
        q2s[:, :, half * (KW // 2):(half + 1) * (KW // 2)] = placed.reshape(
            nd, NM * CAP, KW // 2)
    q2[d] = q2s[d]

    def q2_copy(j):
        dd = (d + j) % nd
        return pltpu.make_async_remote_copy(
            q2s.at[dd], q2.at[d], q2_send.at[j], q2_recv.at[d],
            device_id=(dd, m), device_id_type=MESH)

    def q2_arrival(j):
        dd = (d + j) % nd
        return pltpu.make_async_remote_copy(
            q2s.at[dd], q2.at[dd], q2_send.at[j], q2_recv.at[dd],
            device_id=(dd, m), device_id_type=MESH)

    run(1, nd, lambda j: q2_copy(j).start())

    run(KVH // 2, KVH, suffix_head)

    def sf_copy(j):
        mm = (m + j) % NM
        return pltpu.make_async_remote_copy(
            sfxs.at[mm], sfx.at[m], sf_send.at[j], sf_recv.at[m],
            device_id=(d, mm), device_id_type=MESH)

    def sf_arrival(j):
        mm = (m + j) % NM
        return pltpu.make_async_remote_copy(
            sfxs.at[mm], sfx.at[mm], sf_send.at[j], sf_recv.at[mm],
            device_id=(d, mm), device_id_type=MESH)

    run(1, NM, lambda j: sf_copy(j).start())
    sfx[m] = sfxs[m]

    acc[...] = jnp.zeros_like(acc)
    stat_l[...] = jnp.zeros_like(stat_l)
    stat_m[...] = jnp.full_like(stat_m, FLOOR)
    lse[...] = jnp.zeros_like(lse)
    length = plen_ref[d]
    eye_hd = (iota((HD, HD), 0) == iota((HD, HD), 1)).astype(BF16)
    eye_slot = (iota((nslot, nslot), 0) == iota((nslot, nslot), 1)).astype(BF16)

    def ready(s):
        if s == 0:
            own_k.wait()
            own_v.wait()
        else:
            src_z = (z + s // 2) % 4
            src_y = (y + 4 + (s % 2) * (2 * h - 1)) % 4
            for a, (src, dst) in enumerate(((pk_ref, kr), (pv_ref, vr))):
                pltpu.make_async_remote_copy(
                    src.at[:, cols], dst.at[s], kv_send.at[0, a], kv_recv.at[s, a],
                    device_id=(d, 4 * src_z + src_y), device_id_type=MESH).wait_recv()
        vt[s] = dot(eye_hd, vr[s], NT).astype(BF16)

    def prefix_step(s, g):
        src_z = (z + s // 2) % 4
        src_y = (y + 4 + (s % 2) * (2 * h - 1)) % 4
        first = (4 * src_z + src_y) * chunk
        at = pl.ds(pl.multiple_of(g * HD, HD), HD)
        queries = q2[:, :, at].reshape(nslot, HD)
        scores = dot(kr[s], queries, NT) * SCALE2
        valid = iota((chunk, 1), 0) + first < length
        scores = jnp.where(valid, scores, NEG)
        before = stat_m[g]
        top = jnp.maximum(before, jnp.max(scores, axis=0, keepdims=True))
        factor = jnp.exp2(before - top)
        weights = jnp.exp2(scores - top)
        stat_m[g] = top
        stat_l[g] = stat_l[g] * factor + jnp.sum(weights, axis=0, keepdims=True)
        acc[g] = acc[g] * factor + dot(vt[s], weights.astype(BF16))

    run(1, nd, lambda j: q2_arrival(j).wait_recv())
    for s in SLOT_ORDER[:6]:
        ready(s)
        run(0, G, functools.partial(prefix_step, s))
    for s in SLOT_ORDER[6:]:
        ready(s)

    def re_copy(turn, j):
        dd = (d + j) % nd
        return pltpu.make_async_remote_copy(
            resm.at[turn, dd], rres.at[h, d], re_send.at[turn, j], re_recv.at[h, d],
            device_id=(dd, partner if turn == 0 else m), device_id_type=MESH)

    def re_arrival(turn, j):
        dd = (d + j) % nd
        hh = h if turn == 1 else 1 - h
        return pltpu.make_async_remote_copy(
            resm.at[turn, dd], rres.at[hh, dd], re_send.at[turn, j], re_recv.at[hh, dd],
            device_id=(dd, partner if turn == 0 else m), device_id_type=MESH)

    for turn in range(2):
        first_g = (G // 2) * (h if turn == 1 else 1 - h)

        def finish(n):
            g = first_g + n
            for s in SLOT_ORDER[6:]:
                prefix_step(s, g)
            total = stat_l[g]
            some = total > 0.0
            safe = jnp.where(some, total, 1.0)
            mean = (acc[g] / safe).astype(BF16)
            lse[turn, pl.ds(n, 1), :] = jnp.where(some, stat_m[g] + jnp.log2(safe), NEG)
            turned = dot(eye_slot, mean, NT).astype(BF16)
            at = pl.ds(pl.multiple_of(n * HD, HD), HD)
            resm[turn, :, :, at] = turned.reshape(nd, NM * CAP, HD)

        run(0, G // 2, finish)
        high, mid, low = pieces(lse[turn])
        rest = jnp.zeros((HD - 24, nslot), F32)
        rows = jnp.concatenate([high, mid, low, rest], axis=0).astype(BF16)
        turned = dot(eye_slot, rows, NT).astype(BF16)
        resm[turn, :, :, (G // 2) * HD:] = turned.reshape(nd, NM * CAP, HD)
        run(turn, nd, lambda j: re_copy(turn, j).start())
    rres[h, d] = resm[1, d]

    run(1, NM, lambda j: sf_arrival(j).wait_recv())
    for turn in range(2):
        run(turn, nd, lambda j: re_arrival(turn, j).wait_recv())
    picked = [dot(sel[...], rres[n].reshape(nslot, 5 * HD)) for n in range(2)]
    suffix = sfx[...].astype(F32).reshape(NM, G // 2, S_LOC, 2 * HD)
    for g in range(G // 2):
        levels = []
        means = []
        for value in picked:
            o = 4 * HD + g
            levels.append(value[:, o:o + 1] + value[:, o + 8:o + 9] + value[:, o + 16:o + 17])
            means.append(value[:, g * HD:(g + 1) * HD])
        own = suffix[:, g].reshape(NM * S_LOC, 2 * HD)
        levels.append(own[:, HD:HD + 1] + own[:, HD + 1:HD + 2] + own[:, HD + 2:HD + 3])
        means.append(own[:, :HD])
        top = jnp.maximum(jnp.maximum(levels[0], levels[1]), levels[2])
        shares = [jnp.exp2(level - top) for level in levels]
        inverse = 1.0 / (shares[0] + shares[1] + shares[2])
        total = means[0] * (shares[0] * inverse)
        total = total + means[1] * (shares[1] * inverse)
        total = total + means[2] * (shares[2] * inverse)
        att[:, g * HD:(g + 1) * HD] = total.astype(BF16)

    copy_w.wait()
    width = part.shape[3]
    half_d = w.shape[1] // 2

    def rs_copy(n, j):
        mm = (m + j) % NM
        return pltpu.make_async_remote_copy(
            part.at[n, mm], rsb.at[n, m], rs_send.at[n, j], rs_recv.at[n, m],
            device_id=(d, mm), device_id_type=MESH)

    def rs_arrival(n, j):
        mm = (m + j) % NM
        return pltpu.make_async_remote_copy(
            part.at[n, mm], rsb.at[n, mm], rs_send.at[n, j], rs_recv.at[n, mm],
            device_id=(d, mm), device_id_type=MESH)

    blocks = part.shape[0]
    for n in range(blocks):
        halves = [
            dot(att[...], w[:, c * half_d + n * width:c * half_d + (n + 1) * width]).reshape(
                NM, S_LOC, width)
            for c in range(2)
        ]
        part[n] = jnp.concatenate(halves, axis=1).astype(BF16)
        run(1, NM, functools.partial(lambda n, j: rs_copy(n, j).start(), n))
        rsb[n, m] = part[n, m]
    for n in range(blocks):
        run(1, NM, functools.partial(lambda n, j: rs_arrival(n, j).wait_recv(), n))
        total = rsb[n, 0].astype(F32)
        for j in range(1, NM):
            total = total + rsb[n, j].astype(F32)
        for c in range(2):
            out_ref[:, c * half_d + n * width:c * half_d + (n + 1) * width] = total[
                c * S_LOC:(c + 1) * S_LOC].astype(BF16)

    run(1, NM, lambda j: q1_copy(j).wait_send())
    for c in kv_copies:
        c.wait_send()
    run(1, nd, lambda j: q2_copy(j).wait_send())
    run(1, NM, lambda j: sf_copy(j).wait_send())
    for turn in range(2):
        run(turn, nd, lambda j: re_copy(turn, j).wait_send())
    for n in range(blocks):
        run(1, NM, functools.partial(lambda n, j: rs_copy(n, j).wait_send(), n))


def local(
    nd, q_new, k_new, v_new, suffix_keys, suffix_values, suffix_len, prefix_keys, prefix_values,
    prefix_len, sample_prompt, out_weight,
):
    suf = suffix_keys.shape[1]
    chunk = prefix_keys.shape[1]
    width = out_weight.shape[1]
    rows_x = S_LOC * suf + 128
    nslot = nd * NM * CAP
    blocks = 2
    dma = pltpu.SemaphoreType.DMA
    vmem = pltpu.VMEM
    scratch = [
        vmem((rows_x, KVH * HD), BF16),
        vmem((rows_x, KVH * HD), BF16),
        vmem(out_weight.shape, BF16),
        vmem((8, chunk, HD), BF16),
        vmem((8, chunk, HD), BF16),
        vmem((8, HD, chunk), BF16),
        vmem((KVH, 16, KW // 2 + 128), BF16),
        vmem((NM, 16, KW // 2 + 128), BF16),
        vmem((KVH, 64, HD), BF16),
        vmem((nd, NM * CAP, KW), BF16),
        vmem((nd, NM * CAP, KW), BF16),
        vmem((NM * S_LOC, nslot), BF16),
        vmem((G, HD, nslot), F32),
        vmem((G, 1, nslot), F32),
        vmem((G, 1, nslot), F32),
        vmem((2, 8, nslot), F32),
        vmem((2, nd, NM * CAP, 5 * HD), BF16),
        vmem((2, nd, NM * CAP, 5 * HD), BF16),
        vmem((NM, 32, 2 * HD), BF16),
        vmem((NM, 32, 2 * HD), BF16),
        vmem((NM * S_LOC, (G // 2) * HD), BF16),
        vmem((blocks, NM, 16, width // (2 * blocks)), BF16),
        vmem((blocks, NM, 16, width // (2 * blocks)), BF16),
        vmem((rows_x, 64), F32),
        dma((5,)),
        dma((7, 2)),
        dma((8, 2)),
        dma((NM,)), dma((NM,)),
        dma((nd,)), dma((nd,)),
        dma((NM,)), dma((NM,)),
        dma((2, nd)), dma((2, nd)),
        dma((blocks, NM)), dma((blocks, NM)),
    ]
    smem = pl.BlockSpec(memory_space=pltpu.SMEM)
    whole = pl.BlockSpec(memory_space=pltpu.VMEM)
    anywhere = pl.BlockSpec(memory_space=pl.ANY)
    return pl.pallas_call(
        functools.partial(kernel, nd),
        out_shape=jax.ShapeDtypeStruct((S_LOC, width), BF16),
        in_specs=[smem] * 3 + [whole] * 3 + [anywhere] * 5,
        out_specs=whole,
        scratch_shapes=scratch,
        compiler_params=pltpu.CompilerParams(
            collective_id=0, has_side_effects=True, vmem_limit_bytes=48 * 1024 * 1024
        ),
        name="shared_prefix_step",
    )(
        suffix_len, prefix_len, sample_prompt, q_new, k_new, v_new,
        suffix_keys.reshape(S_LOC * suf, KVH * HD), suffix_values.reshape(S_LOC * suf, KVH * HD),
        prefix_keys.reshape(chunk, KVH * HD), prefix_values.reshape(chunk, KVH * HD), out_weight,
    )


def solution(mesh):
    rows = ("dp", "mp")
    in_specs = (
        P(rows, None),
        P(rows, None),
        P(rows, None),
        P(rows, None, None),
        P(rows, None, None),
        P(rows),
        P("dp", "mp", None),
        P("dp", "mp", None),
        P(),
        P(rows),
        P("mp", None),
    )
    return jax.shard_map(
        functools.partial(local, mesh.shape["dp"]), mesh=mesh, in_specs=in_specs,
        out_specs=P(rows, None), check_vma=False)
```

```python
import functools
import math

import jax
import jax.numpy as jnp
from jax import lax
from jax.experimental import pallas as pl
from jax.experimental.pallas import tpu as pltpu
from jax.sharding import PartitionSpec as P

H = 64
KVH = 8
G = H // KVH
HD = 128
CAP = 2
S_LOC = 8
NM = 16
KW = G * HD
NEG = -1e30
FLOOR = -1e28
SCALE2 = HD ** (-0.5) * math.log2(math.e)
PAIRS = ((0, 1), (2, 3), (6, 7), (4, 5))
F32 = jnp.float32
BF16 = jnp.bfloat16
MESH = pl.DeviceIdType.MESH

NT = (((1,), (1,)), ((), ()))
TN = (((0,), (0,)), ((), ()))


def dot(a, b, dims=(((1,), (0,)), ((), ()))):
    return lax.dot_general(a, b, dims, preferred_element_type=F32)


def iota(shape, dim):
    return lax.broadcasted_iota(jnp.int32, shape, dim)


def pieces(value):
    high = value.astype(BF16).astype(F32)
    rest = value - high
    mid = rest.astype(BF16).astype(F32)
    low = (rest - mid).astype(BF16).astype(F32)
    return high, mid, low


def kernel(
    nd, slen_any, plen_any, sp_any, q_any, kn_any, vn_any, sk_ref, sv_ref, pk_ref, pv_ref, w_ref,
    out_any,
    slen_ref, plen_ref, sp_ref, q_ref, kn_ref, vn_ref, out_ref,
    kx, vx, w, ka, va, q1s, q1, qk, q2s, q2, qa, sel, acc, peak, resm, rres,
    sfxs, sfx, att, part, rsb, bias,
    local_sem, kv_send, kv_recv, q1_send, q1_recv, q2_send, q2_recv, sf_send, sf_recv,
    re_send, re_recv, rs_send, rs_recv,
):
    d = lax.axis_index("dp")
    m = lax.axis_index("mp")
    z, y = m // 4, m % 4
    k, h = m // 2, m % 2
    partner = m + 1 - 2 * h
    suf = sk_ref.shape[0] // S_LOC
    rows_own = S_LOC * suf
    rows_x = kx.shape[0]
    chunk = pk_ref.shape[0]
    nslot = nd * NM * CAP

    def settle(ref, sem):
        pltpu.make_async_copy(ref, ref, sem).wait()

    barrier = pltpu.get_barrier_semaphore()

    def greet(dd, mm):
        pl.semaphore_signal(barrier, inc=1, device_id=(dd, mm), device_id_type=MESH)

    def greet_mp(j, c):
        greet(d, (m + j) % NM)
        return c

    def greet_dp(j, c):
        greet((d + j) % nd, m)
        greet((d + j) % nd, partner)
        return c

    lax.fori_loop(1, NM, greet_mp, 0)
    lax.fori_loop(1, nd, greet_dp, 0)

    cols = pl.ds(pl.multiple_of(k * HD, HD), HD)
    own_k = pltpu.make_async_copy(pk_ref.at[:, cols], ka.at[0, :, 0:HD], local_sem.at[0])
    own_v = pltpu.make_async_copy(pv_ref.at[:, cols], va.at[0, :, 0:HD], local_sem.at[1])
    copy_sk = pltpu.make_async_copy(sk_ref, kx.at[pl.ds(0, rows_own)], local_sem.at[2])
    copy_sv = pltpu.make_async_copy(sv_ref, vx.at[pl.ds(0, rows_own)], local_sem.at[3])
    copy_w = pltpu.make_async_copy(w_ref, w, local_sem.at[4])
    small = [
        pltpu.make_async_copy(src, dst, local_sem.at[5 + n])
        for n, (src, dst) in enumerate((
            (sp_any, sp_ref), (q_any, q_ref), (slen_any, slen_ref), (plen_any, plen_ref),
            (kn_any, kn_ref), (vn_any, vn_ref)))
    ]
    for c in small:
        c.start()
    for c in (own_k, own_v, copy_sk, copy_sv, copy_w):
        c.start()

    small[0].wait()
    small[1].wait()

    prompts = [sp_ref[i] for i in range(S_LOC)]
    targets = []
    for i in range(S_LOC):
        rank = jnp.int32(0)
        for j in range(i):
            rank = rank + jnp.where(prompts[j] == prompts[i], 1, 0)
        targets.append(prompts[i] * (NM * CAP) + m * CAP + rank)
    row16 = iota((16, 128), 0) % S_LOC
    target16 = jnp.zeros((16, 128), jnp.int32)
    for i in range(S_LOC):
        target16 = jnp.where(row16 == i, targets[i], target16)
    target16 = target16.astype(F32)

    for kk in range(KVH):
        block = q_ref[:, kk * KW:(kk + 1) * KW].astype(F32)
        both = jnp.concatenate([block[:, : KW // 2], block[:, KW // 2:]], axis=0)
        q1s[kk, :, 0: KW // 2] = both.astype(BF16)
        q1s[kk, :, KW // 2:] = target16.astype(BF16)
        heads = jnp.concatenate([block[:, g * HD:(g + 1) * HD] for g in range(G)], axis=0)
        qk[kk] = heads.astype(BF16)
    q1[m] = q1s[k]

    pl.semaphore_wait(barrier, NM - 1 + 2 * (nd - 1))

    def q1_copy(j):
        mm = (m + j) % NM
        return pltpu.make_async_remote_copy(
            q1s.at[mm // 2], q1.at[m], q1_send, q1_recv, device_id=(d, mm), device_id_type=MESH)

    def run(lo, hi, body):
        def step(j, c):
            body(j)
            return c
        lax.fori_loop(lo, hi, step, 0)

    run(1, NM, lambda j: q1_copy(j).start())

    kv_copies = []
    for n, (tz, t) in enumerate([(0, 1), (1, 0), (1, 1), (3, 0), (3, 1), (2, 0), (2, 1)]):
        zz = (z + tz) % 4
        pair = (y // 2 + t) % 2
        kk = 2 * zz + pair
        rel = (y + 4 - 2 * pair) % 4
        yy = 2 * pair + ((rel + 1) // 2) % 2
        flag = (yy + 4 - y) % 2
        slot = 2 * ((4 - tz) % 4) + flag
        src_cols = pl.ds(pl.multiple_of(kk * HD, HD), HD)
        for a, (src, dst) in enumerate(((pk_ref, ka), (pv_ref, va))):
            kv_copies.append(pltpu.make_async_remote_copy(
                src.at[:, src_cols], dst.at[slot, :, 0:HD], kv_send.at[n, a], kv_recv.at[slot, a],
                device_id=(d, 4 * zz + yy), device_id_type=MESH))
    for c in kv_copies:
        c.start()

    pad = jnp.zeros((rows_x - rows_own - S_LOC, KW), F32)
    for c in small[2:]:
        c.wait()
    copy_sk.wait()
    copy_sv.wait()
    kx[rows_own:, :] = jnp.concatenate([kn_ref[...].astype(F32), pad], axis=0).astype(BF16)
    vx[rows_own:, :] = jnp.concatenate([vn_ref[...].astype(F32), pad], axis=0).astype(BF16)
    lane_sample = iota((suf, 64), 1) % S_LOC
    position = iota((suf, 64), 0)
    for i in range(S_LOC):
        good = jnp.logical_and(lane_sample == i, position < slen_ref[i])
        bias[i * suf:(i + 1) * suf, :] = jnp.where(good, 0.0, NEG)
    tail = (rows_x - rows_own, 64)
    bias[rows_own:, :] = jnp.where(iota(tail, 0) == iota(tail, 1) % S_LOC, 0.0, NEG)
    eye64 = (iota((64, 64), 0) == iota((64, 64), 1)).astype(BF16)

    def suffix_head(kk):
        at = pl.ds(pl.multiple_of(kk * HD, HD), HD)
        scores = dot(kx[:, at], qk[kk], NT) * SCALE2 + bias[...]
        top = jnp.max(scores, axis=0, keepdims=True)
        weights = jnp.exp2(scores - top)
        total = jnp.sum(weights, axis=0, keepdims=True)
        mean = dot(vx[:, at], weights.astype(BF16), TN) / total
        high, mid, low = pieces(top + jnp.log2(total))
        row = iota((HD, 64), 0)
        extra = jnp.where(row == 0, high, jnp.where(row == 1, mid, jnp.where(row == 2, low, 0.0)))
        both = jnp.concatenate([mean, extra], axis=0).astype(BF16)
        turned = dot(eye64, both, NT).astype(BF16)
        sfxs[2 * kk] = turned[:32]
        sfxs[2 * kk + 1] = turned[32:]

    run(0, KVH // 2, suffix_head)

    settle(q1.at[pl.ds(0, NM - 1)], q1_recv)
    arrived = q1[...].astype(F32).reshape(NM, 2, S_LOC, KW // 2 + 128)
    at_slot = arrived[:, 0, :, KW // 2:].reshape(NM * S_LOC, 128)
    lane = iota((NM * S_LOC, 128), 1)
    for part_at in range(nslot // 128):
        sel[:, part_at * 128:(part_at + 1) * 128] = (
            at_slot == (lane + part_at * 128).astype(F32)).astype(F32).astype(BF16)
    for half in range(2):
        mine = arrived[:, half, :, : KW // 2].reshape(NM * S_LOC, KW // 2).astype(BF16)
        placed = dot(sel[...], mine, TN).astype(BF16)
        q2s[:, :, half * (KW // 2):(half + 1) * (KW // 2)] = placed.reshape(
            nd, NM * CAP, KW // 2)
    q2[d] = q2s[d]

    def q2_copy(j):
        dd = (d + j) % nd
        return pltpu.make_async_remote_copy(
            q2s.at[dd], q2.at[d], q2_send, q2_recv, device_id=(dd, m), device_id_type=MESH)

    run(1, nd, lambda j: q2_copy(j).start())

    run(KVH // 2, KVH, suffix_head)

    def sf_copy(j):
        mm = (m + j) % NM
        return pltpu.make_async_remote_copy(
            sfxs.at[mm], sfx.at[m], sf_send, sf_recv, device_id=(d, mm), device_id_type=MESH)

    run(1, NM, lambda j: sf_copy(j).start())
    sfx[m] = sfxs[m]

    acc[...] = jnp.zeros_like(acc)
    peak[...] = jnp.full_like(peak, FLOOR)
    va[:, :, HD:] = jnp.ones((va.shape[0], chunk, HD), BF16)
    length = plen_ref[d]
    rows_u = G * NM * CAP

    def ready(s):
        if s == 0:
            own_k.wait()
            own_v.wait()
        else:
            for a, (src, dst) in enumerate(((pk_ref, ka), (pv_ref, va))):
                pltpu.make_async_copy(
                    src.at[:, cols], dst.at[s, :, 0:HD], kv_recv.at[s, a]).wait()
        ka[s, :, HD:] = ka[s, :, :HD]

    def widen(value, n):
        return jnp.concatenate([value] * n, axis=1)

    def prefix_unit(pair, dd):
        queries = qa[dd]
        tiles = chunk // HD
        scores = []
        for s in pair:
            src_z = (z + s // 2) % 4
            src_y = (y + 4 + (s % 2) * (2 * h - 1)) % 4
            valid = iota((1, chunk), 1) + (4 * src_z + src_y) * chunk < length
            scores.append(jnp.where(valid, dot(queries, ka[s], NT), NEG))
        before = peak[dd]
        high = functools.reduce(
            jnp.maximum, [x[:, n * HD:(n + 1) * HD] for x in scores for n in range(tiles)])
        high = jnp.broadcast_to(jnp.max(high, axis=1, keepdims=True), (rows_u, HD))
        top = jnp.maximum(before, high)
        factor = jnp.exp2(before - top)
        peak[dd] = top
        total = acc[dd] * widen(factor, 2)
        for s, x in zip(pair, scores):
            total = total + dot(jnp.exp2(x - widen(top, tiles)).astype(BF16), va[s])
        acc[dd] = total

    def scaled_queries(dd):
        rows = jnp.concatenate(
            [q2[dd, :, g * HD:(g + 1) * HD].astype(F32) for g in range(G)], axis=0) * SCALE2
        top = rows.astype(BF16)
        qa[dd, :, :HD] = top
        qa[dd, :, HD:] = (rows - top.astype(F32)).astype(BF16)

    def finish(dd):
        value = acc[dd]
        total = value[:, HD:]
        some = total > 0.0
        safe = jnp.where(some, total, 1.0)
        mean = (value[:, :HD] / safe).astype(BF16)
        level = jnp.where(some, peak[dd] + jnp.log2(safe), NEG)
        lane = iota((NM * CAP, HD), 1)
        for j in range(2):
            mix = jnp.zeros((NM * CAP, HD), F32)
            for n in range(G // 2):
                at = (j * (G // 2) + n) * NM * CAP
                resm[j, dd, :, n * HD:(n + 1) * HD] = mean[at:at + NM * CAP]
                mix = jnp.where(lane % 8 == n, level[at:at + NM * CAP], mix)
            high, mid, low = pieces(mix)
            mix = jnp.where(lane < 8, high, jnp.where(lane < 16, mid, low))
            resm[j, dd, :, (G // 2) * HD:] = jnp.where(lane < 24, mix, 0.0).astype(BF16)

    def re_copy(j, dd):
        return pltpu.make_async_remote_copy(
            resm.at[j, dd], rres.at[h * nd + d], re_send, re_recv,
            device_id=(dd, 2 * k + j), device_id_type=MESH)

    settle(q2.at[pl.ds(0, nd - 1)], q2_recv)
    run(0, nd, scaled_queries)
    for pair in PAIRS[:-1]:
        for s in pair:
            ready(s)
        for dd in range(nd):
            prefix_unit(pair, dd)
    for s in PAIRS[-1]:
        ready(s)
    for t in range(1, nd + 1, 2):
        turn = [(d + t + u) % nd for u in range(2)]
        for dd in turn:
            prefix_unit(PAIRS[-1], dd)
        for u, dd in enumerate(turn):
            finish(dd)
            if t + u < nd:
                for j in range(2):
                    re_copy(j, dd).start()
    re_copy(1 - h, d).start()
    rres[h * nd + d] = resm[h, d]

    settle(sfx.at[pl.ds(0, NM - 1)], sf_recv)
    settle(rres.at[pl.ds(0, 2 * nd - 1)], re_recv)
    picked = [dot(sel[...], rres[n * nd:(n + 1) * nd].reshape(nslot, 5 * HD)) for n in range(2)]
    suffix = sfx[...].astype(F32).reshape(NM, G // 2, S_LOC, 2 * HD)
    for g in range(G // 2):
        levels = []
        means = []
        for value in picked:
            o = 4 * HD + g
            levels.append(value[:, o:o + 1] + value[:, o + 8:o + 9] + value[:, o + 16:o + 17])
            means.append(value[:, g * HD:(g + 1) * HD])
        own = suffix[:, g].reshape(NM * S_LOC, 2 * HD)
        levels.append(own[:, HD:HD + 1] + own[:, HD + 1:HD + 2] + own[:, HD + 2:HD + 3])
        means.append(own[:, :HD])
        top = jnp.maximum(jnp.maximum(levels[0], levels[1]), levels[2])
        shares = [jnp.exp2(level - top) for level in levels]
        inverse = 1.0 / (shares[0] + shares[1] + shares[2])
        total = means[0] * (shares[0] * inverse)
        total = total + means[1] * (shares[1] * inverse)
        total = total + means[2] * (shares[2] * inverse)
        att[:, g * HD:(g + 1) * HD] = total.astype(BF16)

    copy_w.wait()
    width = part.shape[3]
    half_d = w.shape[1] // 2

    def rs_copy(n, j):
        mm = (m + j) % NM
        return pltpu.make_async_remote_copy(
            part.at[n, mm], rsb.at[n, m], rs_send.at[n], rs_recv.at[n],
            device_id=(d, mm), device_id_type=MESH)

    blocks = part.shape[0]
    for n in range(blocks):
        halves = [
            dot(att[...], w[:, c * half_d + n * width:c * half_d + (n + 1) * width]).reshape(
                NM, S_LOC, width)
            for c in range(2)
        ]
        part[n] = jnp.concatenate(halves, axis=1).astype(BF16)
        run(1, NM, functools.partial(lambda n, j: rs_copy(n, j).start(), n))
        rsb[n, m] = part[n, m]
    for n in range(blocks):
        settle(rsb.at[n, pl.ds(0, NM - 1)], rs_recv.at[n])
        total = rsb[n, 0].astype(F32)
        for j in range(1, NM):
            total = total + rsb[n, j].astype(F32)
        for c in range(2):
            out_ref[:, c * half_d + n * width:c * half_d + (n + 1) * width] = total[
                c * S_LOC:(c + 1) * S_LOC].astype(BF16)

    copy_out = pltpu.make_async_copy(out_ref, out_any, local_sem.at[11])
    copy_out.start()
    copy_out.wait()

    settle(q1.at[pl.ds(0, NM - 1)], q1_send)
    for c in kv_copies:
        c.wait_send()
    settle(q2.at[pl.ds(0, nd - 1)], q2_send)
    settle(sfx.at[pl.ds(0, NM - 1)], sf_send)
    settle(rres.at[pl.ds(0, 2 * nd - 1)], re_send)
    for n in range(blocks):
        settle(rsb.at[n, pl.ds(0, NM - 1)], rs_send.at[n])


def local(
    nd, q_new, k_new, v_new, suffix_keys, suffix_values, suffix_len, prefix_keys, prefix_values,
    prefix_len, sample_prompt, out_weight,
):
    suf = suffix_keys.shape[1]
    chunk = prefix_keys.shape[1]
    width = out_weight.shape[1]
    rows_x = S_LOC * suf + 128
    nslot = nd * NM * CAP
    blocks = 2
    dma = pltpu.SemaphoreType.DMA
    vmem = pltpu.VMEM
    smem = pltpu.SMEM
    scratch = [
        smem(suffix_len.shape, jnp.int32),
        smem(prefix_len.shape, jnp.int32),
        smem(sample_prompt.shape, jnp.int32),
        vmem(q_new.shape, BF16),
        vmem(k_new.shape, BF16),
        vmem(v_new.shape, BF16),
        vmem((S_LOC, width), BF16),
        vmem((rows_x, KVH * HD), BF16),
        vmem((rows_x, KVH * HD), BF16),
        vmem(out_weight.shape, BF16),
        vmem((8, chunk, 2 * HD), BF16),
        vmem((8, chunk, 2 * HD), BF16),
        vmem((KVH, 16, KW // 2 + 128), BF16),
        vmem((NM, 16, KW // 2 + 128), BF16),
        vmem((KVH, 64, HD), BF16),
        vmem((nd, NM * CAP, KW), BF16),
        vmem((nd, NM * CAP, KW), BF16),
        vmem((nd, G * NM * CAP, 2 * HD), BF16),
        vmem((NM * S_LOC, nslot), BF16),
        vmem((nd, G * NM * CAP, 2 * HD), F32),
        vmem((nd, G * NM * CAP, HD), F32),
        vmem((2, nd, NM * CAP, 5 * HD), BF16),
        vmem((2 * nd, NM * CAP, 5 * HD), BF16),
        vmem((NM, 32, 2 * HD), BF16),
        vmem((NM, 32, 2 * HD), BF16),
        vmem((NM * S_LOC, (G // 2) * HD), BF16),
        vmem((blocks, NM, 16, width // (2 * blocks)), BF16),
        vmem((blocks, NM, 16, width // (2 * blocks)), BF16),
        vmem((rows_x, 64), F32),
        dma((12,)),
        dma((7, 2)),
        dma((8, 2)),
        dma, dma,
        dma, dma,
        dma, dma,
        dma, dma,
        dma((blocks,)), dma((blocks,)),
    ]
    anywhere = pl.BlockSpec(memory_space=pl.ANY)
    return pl.pallas_call(
        functools.partial(kernel, nd),
        out_shape=jax.ShapeDtypeStruct((S_LOC, width), BF16),
        in_specs=[anywhere] * 11,
        out_specs=anywhere,
        scratch_shapes=scratch,
        compiler_params=pltpu.CompilerParams(
            collective_id=0, has_side_effects=True, vmem_limit_bytes=63 * 1024 * 1024
        ),
        name="shared_prefix_step",
    )(
        suffix_len, prefix_len, sample_prompt, q_new, k_new, v_new,
        suffix_keys.reshape(S_LOC * suf, KVH * HD), suffix_values.reshape(S_LOC * suf, KVH * HD),
        prefix_keys.reshape(chunk, KVH * HD), prefix_values.reshape(chunk, KVH * HD), out_weight,
    )


def solution(mesh):
    rows = ("dp", "mp")
    in_specs = (
        P(rows, None),
        P(rows, None),
        P(rows, None),
        P(rows, None, None),
        P(rows, None, None),
        P(rows),
        P("dp", "mp", None),
        P("dp", "mp", None),
        P(),
        P(rows),
        P("mp", None),
    )
    return jax.shard_map(
        functools.partial(local, mesh.shape["dp"]), mesh=mesh, in_specs=in_specs,
        out_specs=P(rows, None), check_vma=False)
```

```python
import functools
import math

import jax
import jax.numpy as jnp
from jax import lax
from jax.experimental import pallas as pl
from jax.experimental.pallas import tpu as pltpu
from jax.sharding import PartitionSpec as P

H = 64
KVH = 8
G = H // KVH
HD = 128
CAP = 2
S_LOC = 8
NM = 16
KW = G * HD
NEG = -1e30
FLOOR = -1e28
SCALE2 = HD ** (-0.5) * math.log2(math.e)
WHOLE = ((0, 0), (1, 0), (3, 0), (0, 1), (0, 3))
HALVES = (((1, 1), (3, 3)), ((1, 3), (3, 1)), ((0, 2), (2, 0)))
ARRIVAL = ((0, 1, 7), (2, 6, 3, 5, 4))
EARLY = 8
BATCHES = ((0, 1), (2, 3), (4, 5, 6, 7))
F32 = jnp.float32
BF16 = jnp.bfloat16
MESH = pl.DeviceIdType.MESH

NT = (((1,), (1,)), ((), ()))
TN = (((0,), (0,)), ((), ()))


def dot(a, b, dims=(((1,), (0,)), ((), ()))):
    return lax.dot_general(a, b, dims, preferred_element_type=F32)


def half_of(y):
    return ((y + 1) // 2) % 2


def head_of(z, y):
    return 2 * ((z + 2 * half_of(y)) % 4) + y % 2


def iota(shape, dim):
    return lax.broadcasted_iota(jnp.int32, shape, dim)


def pieces(value):
    high = value.astype(BF16).astype(F32)
    rest = value - high
    mid = rest.astype(BF16).astype(F32)
    low = (rest - mid).astype(BF16).astype(F32)
    return high, mid, low


def kernel(
    nd, slen_any, plen_any, sp_any, q_any, kn_any, vn_any, sk_ref, sv_ref, pk_ref, pv_ref, w_ref,
    out_any,
    slen_ref, plen_ref, sp_ref, q_ref, kn_ref, vn_ref, out_ref,
    kx, vx, w, ka, va, q1s, q1, qk, q2s, q2, qa, sel, acc, peak, resm, rres,
    sfxs, sfx, att, part, got, mids, last, bias,
    local_sem, kv_send, kv_recv, q1_send, q1_recv, q2_send, q2_recv, sf_send, sf_recv,
    re_send, re_recv, rs_send, rs_recv,
):
    d = lax.axis_index("dp")
    m = lax.axis_index("mp")
    z, y = m // 4, m % 4
    k, h, b = head_of(z, y), half_of(y), y % 2
    suf = sk_ref.shape[0] // S_LOC
    rows_own = S_LOC * suf
    rows_x = kx.shape[0]
    chunk = pk_ref.shape[0]
    nslot = nd * NM * CAP

    def settle(ref, sem):
        pltpu.make_async_copy(ref, ref, sem).wait()

    barrier = pltpu.get_barrier_semaphore()

    def greet(dd, mm):
        pl.semaphore_signal(barrier, inc=1, device_id=(dd, mm), device_id_type=MESH)

    def greet_mp(j, c):
        greet(d, (m + j) % NM)
        return c

    def greet_dp(j, c):
        for zz, yy in ((z, y), (z, y + 1 - 2 * b), ((z + 2) % 4, (y + 2) % 4), ((z + 2) % 4, 3 - y)):
            greet((d + j) % nd, 4 * zz + yy)
        return c

    lax.fori_loop(1, NM, greet_mp, 0)
    lax.fori_loop(1, nd, greet_dp, 0)

    cols = pl.ds(pl.multiple_of(k * HD, HD), HD)
    own_k = pltpu.make_async_copy(pk_ref.at[:, cols], ka.at[0, :, 0:HD], local_sem.at[0])
    own_v = pltpu.make_async_copy(pv_ref.at[:, cols], va.at[0, :, 0:HD], local_sem.at[1])
    copy_sk = pltpu.make_async_copy(sk_ref, kx.at[pl.ds(0, rows_own)], local_sem.at[2])
    copy_sv = pltpu.make_async_copy(sv_ref, vx.at[pl.ds(0, rows_own)], local_sem.at[3])
    copy_w = pltpu.make_async_copy(w_ref, w, local_sem.at[4])
    small = [
        pltpu.make_async_copy(src, dst, local_sem.at[5 + n])
        for n, (src, dst) in enumerate((
            (sp_any, sp_ref), (q_any, q_ref), (slen_any, slen_ref), (plen_any, plen_ref),
            (kn_any, kn_ref), (vn_any, vn_ref)))
    ]
    for c in small:
        c.start()
    for c in (own_k, own_v, copy_sk, copy_sv, copy_w):
        c.start()

    small[0].wait()
    small[1].wait()

    prompts = [sp_ref[i] for i in range(S_LOC)]
    targets = []
    for i in range(S_LOC):
        rank = jnp.int32(0)
        for j in range(i):
            rank = rank + jnp.where(prompts[j] == prompts[i], 1, 0)
        targets.append(prompts[i] * (NM * CAP) + m * CAP + rank)
    row16 = iota((16, 128), 0) % S_LOC
    target16 = jnp.zeros((16, 128), jnp.int32)
    for i in range(S_LOC):
        target16 = jnp.where(row16 == i, targets[i], target16)
    target16 = target16.astype(F32)

    for kk in range(KVH):
        block = q_ref[:, kk * KW:(kk + 1) * KW].astype(F32)
        both = jnp.concatenate([block[:, : KW // 2], block[:, KW // 2:]], axis=0)
        q1s[kk, :, 0: KW // 2] = both.astype(BF16)
        q1s[kk, :, KW // 2:] = target16.astype(BF16)
        heads = jnp.concatenate([block[:, g * HD:(g + 1) * HD] for g in range(G)], axis=0)
        qk[kk] = heads.astype(BF16)
    q1[m] = q1s[k]

    pl.semaphore_wait(barrier, NM - 1 + 4 * (nd - 1))

    def q1_copy(j):
        mm = (m + j) % NM
        return pltpu.make_async_remote_copy(
            q1s.at[head_of(mm // 4, mm % 4)], q1.at[m], q1_send, q1_recv, device_id=(d, mm), device_id_type=MESH)

    def run(lo, hi, body):
        def step(j, c):
            body(j)
            return c
        lax.fori_loop(lo, hi, step, 0)

    run(1, NM, lambda j: q1_copy(j).start())

    half = chunk // 2

    def kv_copy(n, slot, offset, at):
        zz, yy = (z + 4 - offset[0]) % 4, (y + 4 - offset[1]) % 4
        src_cols = pl.ds(pl.multiple_of(head_of(zz, yy) * HD, HD), HD)
        src_rows, dst_rows = slice(None), slice(None)
        if at is not None:
            src_rows = pl.ds(pl.multiple_of(half_of(yy) * half, half), half)
            dst_rows = pl.ds(at * half, half)
        return [
            pltpu.make_async_remote_copy(
                src.at[src_rows, src_cols], dst.at[slot, dst_rows, 0:HD],
                kv_send.at[n, a], kv_recv.at[slot, a], device_id=(d, 4 * zz + yy),
                device_id_type=MESH)
            for a, (src, dst) in enumerate(((pk_ref, ka), (pv_ref, va)))
        ]

    kv_copies = []
    for slot in range(1, len(WHOLE)):
        kv_copies += kv_copy(slot - 1, slot, WHOLE[slot], None)
    for n, both in enumerate(HALVES):
        for at, offset in enumerate(both):
            kv_copies += kv_copy(len(WHOLE) - 1 + 2 * n + at, len(WHOLE) + n, offset, at)
    for c in kv_copies[:EARLY]:
        c.start()

    pad = jnp.zeros((rows_x - rows_own - S_LOC, KW), F32)
    for c in small[2:]:
        c.wait()
    copy_sk.wait()
    copy_sv.wait()
    kx[rows_own:, :] = jnp.concatenate([kn_ref[...].astype(F32), pad], axis=0).astype(BF16)
    vx[rows_own:, :] = jnp.concatenate([vn_ref[...].astype(F32), pad], axis=0).astype(BF16)
    lane_sample = iota((suf, 64), 1) % S_LOC
    position = iota((suf, 64), 0)
    for i in range(S_LOC):
        good = jnp.logical_and(lane_sample == i, position < slen_ref[i])
        bias[i * suf:(i + 1) * suf, :] = jnp.where(good, 0.0, NEG)
    tail = (rows_x - rows_own, 64)
    bias[rows_own:, :] = jnp.where(iota(tail, 0) == iota(tail, 1) % S_LOC, 0.0, NEG)
    eye64 = (iota((64, 64), 0) == iota((64, 64), 1)).astype(BF16)

    def suffix_head(kk):
        at = pl.ds(pl.multiple_of(kk * HD, HD), HD)
        scores = dot(kx[:, at], qk[kk], NT) * SCALE2 + bias[...]
        top = jnp.max(scores, axis=0, keepdims=True)
        weights = jnp.exp2(scores - top)
        total = jnp.sum(weights, axis=0, keepdims=True)
        mean = dot(vx[:, at], weights.astype(BF16), TN) / total
        high, mid, low = pieces(top + jnp.log2(total))
        row = iota((HD, 64), 0)
        extra = jnp.where(row == 0, high, jnp.where(row == 1, mid, jnp.where(row == 2, low, 0.0)))
        both = jnp.concatenate([mean, extra], axis=0).astype(BF16)
        turned = dot(eye64, both, NT).astype(BF16)
        sfxs[2 * kk] = turned[:32]
        sfxs[2 * kk + 1] = turned[32:]

    run(0, KVH // 2, suffix_head)

    settle(q1.at[pl.ds(0, NM - 1)], q1_recv)
    arrived = q1[...].astype(F32).reshape(NM, 2, S_LOC, KW // 2 + 128)
    at_slot = arrived[:, 0, :, KW // 2:].reshape(NM * S_LOC, 128)
    lane = iota((NM * S_LOC, 128), 1)
    for part_at in range(nslot // 128):
        sel[:, part_at * 128:(part_at + 1) * 128] = (
            at_slot == (lane + part_at * 128).astype(F32)).astype(F32).astype(BF16)
    for side in range(2):
        mine = arrived[:, side, :, : KW // 2].reshape(NM * S_LOC, KW // 2).astype(BF16)
        placed = dot(sel[...], mine, TN).astype(BF16)
        q2s[:, :, side * (KW // 2):(side + 1) * (KW // 2)] = placed.reshape(
            nd, NM * CAP, KW // 2)
    q2[d] = q2s[d]

    def q2_copy(j):
        dd = (d + j) % nd
        return pltpu.make_async_remote_copy(
            q2s.at[dd], q2.at[d], q2_send, q2_recv.at[(nd - j) % nd], device_id=(dd, m), device_id_type=MESH)

    run(1, nd, lambda j: q2_copy(j).start())
    for c in kv_copies[EARLY:]:
        c.start()

    run(KVH // 2, KVH, suffix_head)

    def sf_copy(j):
        mm = (m + j) % NM
        return pltpu.make_async_remote_copy(
            sfxs.at[mm], sfx.at[m], sf_send, sf_recv, device_id=(d, mm), device_id_type=MESH)

    run(1, NM, lambda j: sf_copy(j).start())
    sfx[m] = sfxs[m]

    acc[...] = jnp.zeros_like(acc)
    peak[...] = jnp.full_like(peak, FLOOR)
    va[:, :, HD:] = jnp.ones((va.shape[0], chunk, HD), BF16)
    length = plen_ref[d]
    rows_u = G * NM * CAP

    def ready(s):
        if s == 0:
            own_k.wait()
            own_v.wait()
        else:
            for a, (src, dst) in enumerate(((pk_ref, ka), (pv_ref, va))):
                pltpu.make_async_copy(
                    src.at[:, cols], dst.at[s, :, 0:HD], kv_recv.at[s, a]).wait()
        ka[s, :, HD:] = ka[s, :, :HD]

    def widen(value, n):
        return jnp.concatenate([value] * n, axis=1)

    def positions(s):
        lane = iota((1, chunk), 1)
        if s < len(WHOLE):
            return lane + first_of(WHOLE[s])
        one, two = HALVES[s - len(WHOLE)]
        return jnp.where(
            lane < half, lane + (first_of(one) + h * half), lane + (first_of(two) + (h - 1) * half))

    def first_of(offset):
        return (4 * ((z + offset[0]) % 4) + (y + offset[1]) % 4) * chunk

    def prefix_unit(pair, dd):
        queries = qa[dd]
        tiles = chunk // HD
        scores = []
        for s in pair:
            valid = positions(s) < length
            scores.append(jnp.where(valid, dot(queries, ka[s], NT), NEG))
        before = peak[dd]
        high = functools.reduce(
            jnp.maximum, [x[:, n * HD:(n + 1) * HD] for x in scores for n in range(tiles)])
        high = jnp.broadcast_to(jnp.max(high, axis=1, keepdims=True), (rows_u, HD))
        top = jnp.maximum(before, high)
        factor = jnp.exp2(before - top)
        peak[dd] = top
        total = acc[dd] * widen(factor, 2)
        for s, x in zip(pair, scores):
            total = total + dot(jnp.exp2(x - widen(top, tiles)).astype(BF16), va[s])
        acc[dd] = total

    def scaled_queries(dd):
        rows = jnp.concatenate(
            [q2[dd, :, g * HD:(g + 1) * HD].astype(F32) for g in range(G)], axis=0) * SCALE2
        top = rows.astype(BF16)
        qa[dd, :, :HD] = top
        qa[dd, :, HD:] = (rows - top.astype(F32)).astype(BF16)

    def finish(dd):
        value = acc[dd]
        total = value[:, HD:]
        some = total > 0.0
        safe = jnp.where(some, total, 1.0)
        mean = (value[:, :HD] / safe).astype(BF16)
        level = jnp.where(some, peak[dd] + jnp.log2(safe), NEG)
        lane = iota((NM * CAP, HD), 1)
        for j in range(2):
            mix = jnp.zeros((NM * CAP, HD), F32)
            for n in range(G // 2):
                at = (j * (G // 2) + n) * NM * CAP
                resm[j, dd, :, n * HD:(n + 1) * HD] = mean[at:at + NM * CAP]
                mix = jnp.where(lane % 8 == n, level[at:at + NM * CAP], mix)
            high, mid, low = pieces(mix)
            mix = jnp.where(lane < 8, high, jnp.where(lane < 16, mid, low))
            resm[j, dd, :, (G // 2) * HD:] = jnp.where(lane < 24, mix, 0.0).astype(BF16)

    def re_copy(j, dd):
        return pltpu.make_async_remote_copy(
            resm.at[j, dd], rres.at[h * nd + d], re_send, re_recv,
            device_id=(dd, 2 * k + j), device_id_type=MESH)

    for n, pair in enumerate(BATCHES[:-1]):
        for s in pair:
            ready(s)
        for group in ARRIVAL:
            units = [(d + j) % nd for j in group]
            if n == 0:
                for j, dd in zip(group, units):
                    if j:
                        settle(q2.at[dd], q2_recv.at[j])
                    scaled_queries(dd)
            for dd in units:
                prefix_unit(pair, dd)
    for s in BATCHES[-1]:
        ready(s)
    for t in range(1, nd + 1, 2):
        turn = [(d + t + u) % nd for u in range(2)]
        for dd in turn:
            prefix_unit(BATCHES[-1], dd)
        for u, dd in enumerate(turn):
            finish(dd)
            if t + u < nd:
                for j in range(2):
                    re_copy(j, dd).start()
    re_copy(1 - b, d).start()

    @pl.when(h == 0)
    def _():
        pltpu.make_async_copy(resm.at[b, d], rres.at[d], re_recv).start()

    @pl.when(h == 1)
    def _():
        re_copy(b, d).start()

    settle(sfx.at[pl.ds(0, NM - 1)], sf_recv)
    settle(rres, re_recv)
    picked = [dot(sel[...], rres[n * nd:(n + 1) * nd].reshape(nslot, 5 * HD)) for n in range(2)]
    suffix = sfx[...].astype(F32).reshape(NM, G // 2, S_LOC, 2 * HD)
    for g in range(G // 2):
        levels = []
        means = []
        for value in picked:
            o = 4 * HD + g
            levels.append(value[:, o:o + 1] + value[:, o + 8:o + 9] + value[:, o + 16:o + 17])
            means.append(value[:, g * HD:(g + 1) * HD])
        own = suffix[:, g].reshape(NM * S_LOC, 2 * HD)
        levels.append(own[:, HD:HD + 1] + own[:, HD + 1:HD + 2] + own[:, HD + 2:HD + 3])
        means.append(own[:, :HD])
        top = jnp.maximum(jnp.maximum(levels[0], levels[1]), levels[2])
        shares = [jnp.exp2(level - top) for level in levels]
        inverse = 1.0 / (shares[0] + shares[1] + shares[2])
        total = means[0] * (shares[0] * inverse)
        total = total + means[1] * (shares[1] * inverse)
        total = total + means[2] * (shares[2] * inverse)
        att[:, g * HD:(g + 1) * HD] = total.astype(BF16)

    copy_w.wait()
    blocks, width = part.shape[0], part.shape[4]
    half_d = w.shape[1] // 2

    def along(n, turn):
        if (n + turn) % 2 == 0:
            return y, lambda t: (d, 4 * z + t)
        return z, lambda t: (d, 4 * t + y)

    def rs_copy(n, turn, step):
        here, device = along(n, turn)
        there = (here + step) % 4
        src, dst = ((part, got), (mids, last))[turn]
        return pltpu.make_async_remote_copy(
            src.at[n, there], dst.at[n, here], rs_send.at[n, turn], rs_recv.at[n, turn],
            device_id=device(there), device_id_type=MESH)

    def gathered(n, turn):
        here, _ = along(n, turn)
        src, dst = ((part, got), (mids, last))[turn]
        settle(dst.at[n, pl.ds(0, 3)], rs_recv.at[n, turn])
        total = src[n, here].astype(F32)
        for step in range(1, 4):
            total = total + dst[n, (here + step) % 4].astype(F32)
        return total

    for n in range(blocks):
        halves = [
            dot(att[...], w[:, c * half_d + n * width:c * half_d + (n + 1) * width]).reshape(
                NM, S_LOC, width)
            for c in range(2)
        ]
        value = jnp.concatenate(halves, axis=1).astype(BF16).reshape(4, 4, 2 * S_LOC, width)
        for t in range(4):
            part[n, t] = value[:, t] if n % 2 == 0 else value[t]
        for step in range(1, 4):
            rs_copy(n, 0, step).start()
    for n in range(blocks):
        mids[n] = gathered(n, 0).astype(BF16)
        for step in range(1, 4):
            rs_copy(n, 1, step).start()
    for n in range(blocks):
        total = gathered(n, 1)
        for c in range(2):
            out_ref[:, c * half_d + n * width:c * half_d + (n + 1) * width] = total[
                c * S_LOC:(c + 1) * S_LOC].astype(BF16)

    copy_out = pltpu.make_async_copy(out_ref, out_any, local_sem.at[11])
    copy_out.start()
    copy_out.wait()

    settle(q1.at[pl.ds(0, NM - 1)], q1_send)
    for c in kv_copies:
        c.wait_send()
    settle(q2.at[pl.ds(0, nd - 1)], q2_send)
    settle(sfx.at[pl.ds(0, NM - 1)], sf_send)
    settle(rres.at[pl.ds(0, 2 * nd - 1)], re_send)

    @pl.when(h == 1)
    def _():
        settle(rres.at[0], re_send)

    for n in range(blocks):
        settle(got.at[n, pl.ds(0, 3)], rs_send.at[n, 0])
        settle(last.at[n, pl.ds(0, 3)], rs_send.at[n, 1])


def local(
    nd, q_new, k_new, v_new, suffix_keys, suffix_values, suffix_len, prefix_keys, prefix_values,
    prefix_len, sample_prompt, out_weight,
):
    suf = suffix_keys.shape[1]
    chunk = prefix_keys.shape[1]
    width = out_weight.shape[1]
    rows_x = S_LOC * suf + 128
    nslot = nd * NM * CAP
    blocks = 4
    dma = pltpu.SemaphoreType.DMA
    vmem = pltpu.VMEM
    smem = pltpu.SMEM
    scratch = [
        smem(suffix_len.shape, jnp.int32),
        smem(prefix_len.shape, jnp.int32),
        smem(sample_prompt.shape, jnp.int32),
        vmem(q_new.shape, BF16),
        vmem(k_new.shape, BF16),
        vmem(v_new.shape, BF16),
        vmem((S_LOC, width), BF16),
        vmem((rows_x, KVH * HD), BF16),
        vmem((rows_x, KVH * HD), BF16),
        vmem(out_weight.shape, BF16),
        vmem((8, chunk, 2 * HD), BF16),
        vmem((8, chunk, 2 * HD), BF16),
        vmem((KVH, 16, KW // 2 + 128), BF16),
        vmem((NM, 16, KW // 2 + 128), BF16),
        vmem((KVH, 64, HD), BF16),
        vmem((nd, NM * CAP, KW), BF16),
        vmem((nd, NM * CAP, KW), BF16),
        vmem((nd, G * NM * CAP, 2 * HD), BF16),
        vmem((NM * S_LOC, nslot), BF16),
        vmem((nd, G * NM * CAP, 2 * HD), F32),
        vmem((nd, G * NM * CAP, HD), F32),
        vmem((2, nd, NM * CAP, 5 * HD), BF16),
        vmem((2 * nd, NM * CAP, 5 * HD), BF16),
        vmem((NM, 32, 2 * HD), BF16),
        vmem((NM, 32, 2 * HD), BF16),
        vmem((NM * S_LOC, (G // 2) * HD), BF16),
        vmem((blocks, 4, 4, 16, width // (2 * blocks)), BF16),
        vmem((blocks, 4, 4, 16, width // (2 * blocks)), BF16),
        vmem((blocks, 4, 16, width // (2 * blocks)), BF16),
        vmem((blocks, 4, 16, width // (2 * blocks)), BF16),
        vmem((rows_x, 64), F32),
        dma((12,)),
        dma((10, 2)),
        dma((8, 2)),
        dma, dma,
        dma, dma((nd,)),
        dma, dma,
        dma, dma,
        dma((blocks, 2)), dma((blocks, 2)),
    ]
    anywhere = pl.BlockSpec(memory_space=pl.ANY)
    return pl.pallas_call(
        functools.partial(kernel, nd),
        out_shape=jax.ShapeDtypeStruct((S_LOC, width), BF16),
        in_specs=[anywhere] * 11,
        out_specs=anywhere,
        scratch_shapes=scratch,
        compiler_params=pltpu.CompilerParams(
            collective_id=0, has_side_effects=True, vmem_limit_bytes=63 * 1024 * 1024
        ),
        name="shared_prefix_step",
    )(
        suffix_len, prefix_len, sample_prompt, q_new, k_new, v_new,
        suffix_keys.reshape(S_LOC * suf, KVH * HD), suffix_values.reshape(S_LOC * suf, KVH * HD),
        prefix_keys.reshape(chunk, KVH * HD), prefix_values.reshape(chunk, KVH * HD), out_weight,
    )


def solution(mesh):
    rows = ("dp", "mp")
    in_specs = (
        P(rows, None),
        P(rows, None),
        P(rows, None),
        P(rows, None, None),
        P(rows, None, None),
        P(rows),
        P("dp", "mp", None),
        P("dp", "mp", None),
        P(),
        P(rows),
        P("mp", None),
    )
    return jax.shard_map(
        functools.partial(local, mesh.shape["dp"]), mesh=mesh, in_specs=in_specs,
        out_specs=P(rows, None), check_vma=False)
```

```python
import functools
import math

import jax
import jax.numpy as jnp
from jax import lax
from jax.experimental import pallas as pl
from jax.experimental.pallas import tpu as pltpu
from jax.sharding import PartitionSpec as P

H = 64
KVH = 8
G = H // KVH
HD = 128
CAP = 2
S_LOC = 8
NM = 16
KW = G * HD
NEG = -1e30
FLOOR = -1e28
SCALE2 = HD ** (-0.5) * math.log2(math.e)
WHOLE = ((0, 0), (1, 0), (3, 0), (0, 1), (0, 3))
HALVES = (((1, 1), (3, 3)), ((1, 3), (3, 1)), ((0, 2), (2, 0)))
REPLY = ((1, 2), (3, 4), (5, 6), (7, 0))
STEPS = (2, 1, 3)
ARRIVAL = ((0, 1, 7), (2, 6, 3, 5, 4))
EARLY = 8
BATCHES = ((0, 1), (2, 3), (4, 5, 6, 7))
F32 = jnp.float32
BF16 = jnp.bfloat16
MESH = pl.DeviceIdType.MESH

NT = (((1,), (1,)), ((), ()))
TN = (((0,), (0,)), ((), ()))


def dot(a, b, dims=(((1,), (0,)), ((), ()))):
    return lax.dot_general(a, b, dims, preferred_element_type=F32)


def half_of(y):
    return ((y + 1) // 2) % 2


def head_of(z, y):
    return 2 * ((z + 2 * half_of(y)) % 4) + y % 2


def iota(shape, dim):
    return lax.broadcasted_iota(jnp.int32, shape, dim)


def pieces(value):
    high = value.astype(BF16).astype(F32)
    rest = value - high
    mid = rest.astype(BF16).astype(F32)
    low = (rest - mid).astype(BF16).astype(F32)
    return high, mid, low


def kernel(
    nd, slen_any, plen_any, sp_any, q_any, kn_any, vn_any, sk_ref, sv_ref, pk_ref, pv_ref, w_ref,
    out_any,
    slen_ref, plen_ref, sp_ref, q_ref, kn_ref, vn_ref, out_ref,
    kx, vx, w, ka, va, q1s, q1, qk, q2s, q2, qa, sel, acc, peak, resm, rres,
    sfxs, sfx, att, part, got, mids, last, bias,
    local_sem, kv_send, kv_recv, q1_send, q1_recv, q2_send, q2_recv, sf_send, sf_recv,
    re_send, re_recv, rs_send, rs_recv,
):
    d = lax.axis_index("dp")
    m = lax.axis_index("mp")
    z, y = m // 4, m % 4
    k, h, b = head_of(z, y), half_of(y), y % 2
    suf = sk_ref.shape[0] // S_LOC
    rows_own = S_LOC * suf
    rows_x = kx.shape[0]
    chunk = pk_ref.shape[0]
    nslot = nd * NM * CAP

    def settle(ref, sem):
        pltpu.make_async_copy(ref, ref, sem).wait()

    barrier = pltpu.get_barrier_semaphore()

    def greet(dd, mm):
        pl.semaphore_signal(barrier, inc=1, device_id=(dd, mm), device_id_type=MESH)

    def greet_mp(j, c):
        greet(d, (m + j) % NM)
        return c

    def greet_dp(j, c):
        for zz, yy in ((z, y), (z, y + 1 - 2 * b), ((z + 2) % 4, (y + 2) % 4), ((z + 2) % 4, 3 - y)):
            greet((d + j) % nd, 4 * zz + yy)
        return c

    lax.fori_loop(1, NM, greet_mp, 0)
    lax.fori_loop(1, nd, greet_dp, 0)

    cols = pl.ds(pl.multiple_of(k * HD, HD), HD)
    own_k = pltpu.make_async_copy(pk_ref.at[:, cols], ka.at[0, :, 0:HD], local_sem.at[0])
    own_v = pltpu.make_async_copy(pv_ref.at[:, cols], va.at[0, :, 0:HD], local_sem.at[1])
    copy_sk = pltpu.make_async_copy(sk_ref, kx.at[pl.ds(0, rows_own)], local_sem.at[2])
    copy_sv = pltpu.make_async_copy(sv_ref, vx.at[pl.ds(0, rows_own)], local_sem.at[3])
    copy_w = pltpu.make_async_copy(w_ref, w, local_sem.at[4])
    small = [
        pltpu.make_async_copy(src, dst, local_sem.at[5 + n])
        for n, (src, dst) in enumerate((
            (sp_any, sp_ref), (q_any, q_ref), (slen_any, slen_ref), (plen_any, plen_ref),
            (kn_any, kn_ref), (vn_any, vn_ref)))
    ]
    for c in small:
        c.start()
    for c in (own_k, own_v, copy_sk, copy_sv, copy_w):
        c.start()

    small[0].wait()
    small[1].wait()

    prompts = [sp_ref[i] for i in range(S_LOC)]
    targets = []
    for i in range(S_LOC):
        rank = jnp.int32(0)
        for j in range(i):
            rank = rank + jnp.where(prompts[j] == prompts[i], 1, 0)
        targets.append(prompts[i] * (NM * CAP) + m * CAP + rank)
    row16 = iota((16, 128), 0) % S_LOC
    target16 = jnp.zeros((16, 128), jnp.int32)
    for i in range(S_LOC):
        target16 = jnp.where(row16 == i, targets[i], target16)
    target16 = target16.astype(F32)

    for kk in range(KVH):
        block = q_ref[:, kk * KW:(kk + 1) * KW].astype(F32)
        both = jnp.concatenate([block[:, : KW // 2], block[:, KW // 2:]], axis=0)
        q1s[kk, :, 0: KW // 2] = both.astype(BF16)
        q1s[kk, :, KW // 2:] = target16.astype(BF16)
        heads = jnp.concatenate([block[:, g * HD:(g + 1) * HD] for g in range(G)], axis=0)
        qk[kk] = heads.astype(BF16)
    q1[m] = q1s[k]

    pl.semaphore_wait(barrier, NM - 1 + 4 * (nd - 1))

    def q1_copy(j):
        mm = (m + j) % NM
        return pltpu.make_async_remote_copy(
            q1s.at[head_of(mm // 4, mm % 4)], q1.at[m], q1_send, q1_recv, device_id=(d, mm), device_id_type=MESH)

    def run(lo, hi, body):
        def step(j, c):
            body(j)
            return c
        lax.fori_loop(lo, hi, step, 0)

    run(1, NM, lambda j: q1_copy(j).start())

    half = chunk // 2

    def kv_copy(n, slot, offset, at):
        zz, yy = (z + 4 - offset[0]) % 4, (y + 4 - offset[1]) % 4
        src_cols = pl.ds(pl.multiple_of(head_of(zz, yy) * HD, HD), HD)
        src_rows, dst_rows = slice(None), slice(None)
        if at is not None:
            src_rows = pl.ds(pl.multiple_of(half_of(yy) * half, half), half)
            dst_rows = pl.ds(at * half, half)
        return [
            pltpu.make_async_remote_copy(
                src.at[src_rows, src_cols], dst.at[slot, dst_rows, 0:HD],
                kv_send.at[n, a], kv_recv.at[slot, a], device_id=(d, 4 * zz + yy),
                device_id_type=MESH)
            for a, (src, dst) in enumerate(((pk_ref, ka), (pv_ref, va)))
        ]

    kv_copies = []
    for slot in range(1, len(WHOLE)):
        kv_copies += kv_copy(slot - 1, slot, WHOLE[slot], None)
    for n, both in enumerate(HALVES):
        for at, offset in enumerate(both):
            kv_copies += kv_copy(len(WHOLE) - 1 + 2 * n + at, len(WHOLE) + n, offset, at)
    for c in kv_copies[:EARLY]:
        c.start()

    pad = jnp.zeros((rows_x - rows_own - S_LOC, KW), F32)
    for c in small[2:]:
        c.wait()
    copy_sk.wait()
    copy_sv.wait()
    kx[rows_own:, :] = jnp.concatenate([kn_ref[...].astype(F32), pad], axis=0).astype(BF16)
    vx[rows_own:, :] = jnp.concatenate([vn_ref[...].astype(F32), pad], axis=0).astype(BF16)
    lane_sample = iota((suf, 64), 1) % S_LOC
    position = iota((suf, 64), 0)
    for i in range(S_LOC):
        good = jnp.logical_and(lane_sample == i, position < slen_ref[i])
        bias[i * suf:(i + 1) * suf, :] = jnp.where(good, 0.0, NEG)
    tail = (rows_x - rows_own, 64)
    bias[rows_own:, :] = jnp.where(iota(tail, 0) == iota(tail, 1) % S_LOC, 0.0, NEG)
    eye64 = (iota((64, 64), 0) == iota((64, 64), 1)).astype(BF16)

    def suffix_head(kk):
        at = pl.ds(pl.multiple_of(kk * HD, HD), HD)
        scores = dot(kx[:, at], qk[kk], NT) * SCALE2 + bias[...]
        top = jnp.max(scores, axis=0, keepdims=True)
        weights = jnp.exp2(scores - top)
        total = jnp.sum(weights, axis=0, keepdims=True)
        mean = dot(vx[:, at], weights.astype(BF16), TN) / total
        high, mid, low = pieces(top + jnp.log2(total))
        row = iota((HD, 64), 0)
        extra = jnp.where(row == 0, high, jnp.where(row == 1, mid, jnp.where(row == 2, low, 0.0)))
        both = jnp.concatenate([mean, extra], axis=0).astype(BF16)
        turned = dot(eye64, both, NT).astype(BF16)
        sfxs[2 * kk] = turned[:32]
        sfxs[2 * kk + 1] = turned[32:]

    run(0, KVH // 2, suffix_head)

    settle(q1.at[pl.ds(0, NM - 1)], q1_recv)
    arrived = q1[...].astype(F32).reshape(NM, 2, S_LOC, KW // 2 + 128)
    at_slot = arrived[:, 0, :, KW // 2:].reshape(NM * S_LOC, 128)
    lane = iota((NM * S_LOC, 128), 1)
    for part_at in range(nslot // 128):
        sel[:, part_at * 128:(part_at + 1) * 128] = (
            at_slot == (lane + part_at * 128).astype(F32)).astype(F32).astype(BF16)
    for side in range(2):
        mine = arrived[:, side, :, : KW // 2].reshape(NM * S_LOC, KW // 2).astype(BF16)
        placed = dot(sel[...], mine, TN).astype(BF16)
        q2s[:, :, side * (KW // 2):(side + 1) * (KW // 2)] = placed.reshape(
            nd, NM * CAP, KW // 2)
    q2[d] = q2s[d]

    def q2_copy(j):
        dd = (d + j) % nd
        return pltpu.make_async_remote_copy(
            q2s.at[dd], q2.at[d], q2_send, q2_recv.at[(nd - j) % nd], device_id=(dd, m), device_id_type=MESH)

    run(1, nd, lambda j: q2_copy(j).start())
    for c in kv_copies[EARLY:]:
        c.start()

    run(KVH // 2, KVH, suffix_head)

    def sf_copy(j):
        mm = (m + j) % NM
        return pltpu.make_async_remote_copy(
            sfxs.at[mm], sfx.at[m], sf_send, sf_recv, device_id=(d, mm), device_id_type=MESH)

    run(1, NM, lambda j: sf_copy(j).start())
    sfx[m] = sfxs[m]

    acc[...] = jnp.zeros_like(acc)
    peak[...] = jnp.full_like(peak, FLOOR)
    va[:, :, HD:] = jnp.ones((va.shape[0], chunk, HD), BF16)
    length = plen_ref[d]
    rows_u = G * NM * CAP

    def ready(s):
        if s == 0:
            own_k.wait()
            own_v.wait()
        else:
            for a, (src, dst) in enumerate(((pk_ref, ka), (pv_ref, va))):
                pltpu.make_async_copy(
                    src.at[:, cols], dst.at[s, :, 0:HD], kv_recv.at[s, a]).wait()
        ka[s, :, HD:] = ka[s, :, :HD]

    def widen(value, n):
        return jnp.concatenate([value] * n, axis=1)

    def positions(s):
        lane = iota((1, chunk), 1)
        if s < len(WHOLE):
            return lane + first_of(WHOLE[s])
        one, two = HALVES[s - len(WHOLE)]
        return jnp.where(
            lane < half, lane + (first_of(one) + h * half), lane + (first_of(two) + (h - 1) * half))

    def first_of(offset):
        return (4 * ((z + offset[0]) % 4) + (y + offset[1]) % 4) * chunk

    def prefix_unit(pair, dd):
        queries = qa[dd]
        tiles = chunk // HD
        scores = []
        for s in pair:
            valid = positions(s) < length
            scores.append(jnp.where(valid, dot(queries, ka[s], NT), NEG))
        before = peak[dd]
        high = functools.reduce(
            jnp.maximum, [x[:, n * HD:(n + 1) * HD] for x in scores for n in range(tiles)])
        high = jnp.broadcast_to(jnp.max(high, axis=1, keepdims=True), (rows_u, HD))
        top = jnp.maximum(before, high)
        factor = jnp.exp2(before - top)
        peak[dd] = top
        total = acc[dd] * widen(factor, 2)
        for s, x in zip(pair, scores):
            total = total + dot(jnp.exp2(x - widen(top, tiles)).astype(BF16), va[s])
        acc[dd] = total

    def scaled_queries(dd):
        rows = jnp.concatenate(
            [q2[dd, :, g * HD:(g + 1) * HD].astype(F32) for g in range(G)], axis=0) * SCALE2
        top = rows.astype(BF16)
        qa[dd, :, :HD] = top
        qa[dd, :, HD:] = (rows - top.astype(F32)).astype(BF16)

    def finish(dd):
        value = acc[dd]
        total = value[:, HD:]
        some = total > 0.0
        safe = jnp.where(some, total, 1.0)
        mean = (value[:, :HD] / safe).astype(BF16)
        level = jnp.where(some, peak[dd] + jnp.log2(safe), NEG)
        lane = iota((NM * CAP, HD), 1)
        for j in range(2):
            mix = jnp.zeros((NM * CAP, HD), F32)
            for n in range(G // 2):
                at = (j * (G // 2) + n) * NM * CAP
                resm[j, dd, :, n * HD:(n + 1) * HD] = mean[at:at + NM * CAP]
                mix = jnp.where(lane % 8 == n, level[at:at + NM * CAP], mix)
            high, mid, low = pieces(mix)
            mix = jnp.where(lane < 8, high, jnp.where(lane < 16, mid, low))
            resm[j, dd, :, (G // 2) * HD:] = jnp.where(lane < 24, mix, 0.0).astype(BF16)

    def re_copy(j, dd):
        return pltpu.make_async_remote_copy(
            resm.at[j, dd], rres.at[h * nd + d], re_send, re_recv,
            device_id=(dd, 2 * k + j), device_id_type=MESH)

    for n, pair in enumerate(BATCHES[:-1]):
        for s in pair:
            ready(s)
        for group in ARRIVAL:
            units = [(d + j) % nd for j in group]
            if n == 0:
                for j, dd in zip(group, units):
                    if j:
                        settle(q2.at[dd], q2_recv.at[j])
                    scaled_queries(dd)
            for dd in units:
                prefix_unit(pair, dd)
    for s in BATCHES[-1]:
        ready(s)
    for pair in REPLY:
        turn = [(d + j) % nd for j in pair]
        for dd in turn:
            prefix_unit(BATCHES[-1], dd)
        for j, dd in zip(pair, turn):
            finish(dd)
            if j:
                for part_of in range(2):
                    re_copy(part_of, dd).start()
    re_copy(1 - b, d).start()

    @pl.when(h == 0)
    def _():
        pltpu.make_async_copy(resm.at[b, d], rres.at[d], re_recv).start()

    @pl.when(h == 1)
    def _():
        re_copy(b, d).start()

    settle(sfx.at[pl.ds(0, NM - 1)], sf_recv)
    settle(rres, re_recv)
    picked = [dot(sel[...], rres[n * nd:(n + 1) * nd].reshape(nslot, 5 * HD)) for n in range(2)]
    suffix = sfx[...].astype(F32).reshape(NM, G // 2, S_LOC, 2 * HD)
    for g in range(G // 2):
        levels = []
        means = []
        for value in picked:
            o = 4 * HD + g
            levels.append(value[:, o:o + 1] + value[:, o + 8:o + 9] + value[:, o + 16:o + 17])
            means.append(value[:, g * HD:(g + 1) * HD])
        own = suffix[:, g].reshape(NM * S_LOC, 2 * HD)
        levels.append(own[:, HD:HD + 1] + own[:, HD + 1:HD + 2] + own[:, HD + 2:HD + 3])
        means.append(own[:, :HD])
        top = jnp.maximum(jnp.maximum(levels[0], levels[1]), levels[2])
        shares = [jnp.exp2(level - top) for level in levels]
        inverse = 1.0 / (shares[0] + shares[1] + shares[2])
        total = means[0] * (shares[0] * inverse)
        total = total + means[1] * (shares[1] * inverse)
        total = total + means[2] * (shares[2] * inverse)
        att[:, g * HD:(g + 1) * HD] = total.astype(BF16)

    copy_w.wait()
    blocks, width = part.shape[0], part.shape[4]
    half_d = w.shape[1] // 2

    def along(n, turn):
        if (n + turn) % 2 == 0:
            return y, lambda t: (d, 4 * z + t)
        return z, lambda t: (d, 4 * t + y)

    def rs_copy(n, turn, step):
        here, device = along(n, turn)
        there = (here + step) % 4
        src, dst = ((part, got), (mids, last))[turn]
        return pltpu.make_async_remote_copy(
            src.at[n, there], dst.at[n, here], rs_send.at[n, turn], rs_recv.at[n, turn],
            device_id=device(there), device_id_type=MESH)

    def gathered(n, turn):
        here, _ = along(n, turn)
        src, dst = ((part, got), (mids, last))[turn]
        settle(dst.at[n, pl.ds(0, 3)], rs_recv.at[n, turn])
        total = src[n, here].astype(F32)
        for step in range(1, 4):
            total = total + dst[n, (here + step) % 4].astype(F32)
        return total

    for n in range(blocks):
        halves = [
            dot(att[...], w[:, c * half_d + n * width:c * half_d + (n + 1) * width]).reshape(
                NM, S_LOC, width)
            for c in range(2)
        ]
        value = jnp.concatenate(halves, axis=1).astype(BF16).reshape(4, 4, 2 * S_LOC, width)
        for t in range(4):
            part[n, t] = value[:, t] if n % 2 == 0 else value[t]
        for step in STEPS:
            rs_copy(n, 0, step).start()
    for n in range(blocks):
        mids[n] = gathered(n, 0).astype(BF16)
        for step in STEPS:
            rs_copy(n, 1, step).start()
    for n in range(blocks):
        total = gathered(n, 1)
        for c in range(2):
            out_ref[:, c * half_d + n * width:c * half_d + (n + 1) * width] = total[
                c * S_LOC:(c + 1) * S_LOC].astype(BF16)

    copy_out = pltpu.make_async_copy(out_ref, out_any, local_sem.at[11])
    copy_out.start()
    copy_out.wait()

    settle(q1.at[pl.ds(0, NM - 1)], q1_send)
    for c in kv_copies:
        c.wait_send()
    settle(q2.at[pl.ds(0, nd - 1)], q2_send)
    settle(sfx.at[pl.ds(0, NM - 1)], sf_send)
    settle(rres.at[pl.ds(0, 2 * nd - 1)], re_send)

    @pl.when(h == 1)
    def _():
        settle(rres.at[0], re_send)

    for n in range(blocks):
        settle(got.at[n, pl.ds(0, 3)], rs_send.at[n, 0])
        settle(last.at[n, pl.ds(0, 3)], rs_send.at[n, 1])


def local(
    nd, q_new, k_new, v_new, suffix_keys, suffix_values, suffix_len, prefix_keys, prefix_values,
    prefix_len, sample_prompt, out_weight,
):
    suf = suffix_keys.shape[1]
    chunk = prefix_keys.shape[1]
    width = out_weight.shape[1]
    rows_x = S_LOC * suf + 128
    nslot = nd * NM * CAP
    blocks = 10
    dma = pltpu.SemaphoreType.DMA
    vmem = pltpu.VMEM
    smem = pltpu.SMEM
    scratch = [
        smem(suffix_len.shape, jnp.int32),
        smem(prefix_len.shape, jnp.int32),
        smem(sample_prompt.shape, jnp.int32),
        vmem(q_new.shape, BF16),
        vmem(k_new.shape, BF16),
        vmem(v_new.shape, BF16),
        vmem((S_LOC, width), BF16),
        vmem((rows_x, KVH * HD), BF16),
        vmem((rows_x, KVH * HD), BF16),
        vmem(out_weight.shape, BF16),
        vmem((8, chunk, 2 * HD), BF16),
        vmem((8, chunk, 2 * HD), BF16),
        vmem((KVH, 16, KW // 2 + 128), BF16),
        vmem((NM, 16, KW // 2 + 128), BF16),
        vmem((KVH, 64, HD), BF16),
        vmem((nd, NM * CAP, KW), BF16),
        vmem((nd, NM * CAP, KW), BF16),
        vmem((nd, G * NM * CAP, 2 * HD), BF16),
        vmem((NM * S_LOC, nslot), BF16),
        vmem((nd, G * NM * CAP, 2 * HD), F32),
        vmem((nd, G * NM * CAP, HD), F32),
        vmem((2, nd, NM * CAP, 5 * HD), BF16),
        vmem((2 * nd, NM * CAP, 5 * HD), BF16),
        vmem((NM, 32, 2 * HD), BF16),
        vmem((NM, 32, 2 * HD), BF16),
        vmem((NM * S_LOC, (G // 2) * HD), BF16),
        vmem((blocks, 4, 4, 16, width // (2 * blocks)), BF16),
        vmem((blocks, 4, 4, 16, width // (2 * blocks)), BF16),
        vmem((blocks, 4, 16, width // (2 * blocks)), BF16),
        vmem((blocks, 4, 16, width // (2 * blocks)), BF16),
        vmem((rows_x, 64), F32),
        dma((12,)),
        dma((10, 2)),
        dma((8, 2)),
        dma, dma,
        dma, dma((nd,)),
        dma, dma,
        dma, dma,
        dma((blocks, 2)), dma((blocks, 2)),
    ]
    anywhere = pl.BlockSpec(memory_space=pl.ANY)
    return pl.pallas_call(
        functools.partial(kernel, nd),
        out_shape=jax.ShapeDtypeStruct((S_LOC, width), BF16),
        in_specs=[anywhere] * 11,
        out_specs=anywhere,
        scratch_shapes=scratch,
        compiler_params=pltpu.CompilerParams(
            collective_id=0, has_side_effects=True, vmem_limit_bytes=63 * 1024 * 1024
        ),
        name="shared_prefix_step",
    )(
        suffix_len, prefix_len, sample_prompt, q_new, k_new, v_new,
        suffix_keys.reshape(S_LOC * suf, KVH * HD), suffix_values.reshape(S_LOC * suf, KVH * HD),
        prefix_keys.reshape(chunk, KVH * HD), prefix_values.reshape(chunk, KVH * HD), out_weight,
    )


def solution(mesh):
    rows = ("dp", "mp")
    in_specs = (
        P(rows, None),
        P(rows, None),
        P(rows, None),
        P(rows, None, None),
        P(rows, None, None),
        P(rows),
        P("dp", "mp", None),
        P("dp", "mp", None),
        P(),
        P(rows),
        P("mp", None),
    )
    return jax.shard_map(
        functools.partial(local, mesh.shape["dp"]), mesh=mesh, in_specs=in_specs,
        out_specs=P(rows, None), check_vma=False)
```
